1024 devices in a mesh: dp: 128 (over z, y), opt: 8 (over x, core).
Axes of the slice: x: 4, y: 4, z: 32, core: 2. Of those that a mesh axis runs over, the one named last changes fastest.
Arguments:
- activations: bfloat16 [262144, 1024], P(('dp', 'opt')), may hold values from -24 to 24
- hidden_grad: bfloat16 [262144, 8, 384], P(('dp', 'opt')), may hold values from -6 to 6
- routing: int32 [262144, 8], P(('dp', 'opt')), may hold values from 0 to 127, all different within a row; in each aligned block of 256 rows (0 to 255, 256 to 511, ...) at most 32 rows name the same one
- momentum: float32 [8, 1024, 384], P('opt', 'dp'), may hold values from -600 to 600
- master: float32 [8, 1024, 384], P('opt', 'dp'), may hold values from -6 to 6
Outputs:
- momentum_out: float32 [8, 1024, 384], P('opt', 'dp')
- master_out: float32 [8, 1024, 384], P('opt', 'dp')
- update: float32 [8, 1024, 384], P('opt', 'dp')
The draws below stay inside these ranges and needn't reach their ends.
Inputs may be any that keep to these rules, and one draw needn't show every extreme that they name: `routing`: each row names 8 different experts. Among the 256 rows of one device, at most 32 name any one expert.
All inputs are finite; a program needn't handle non-finite values.
Results may differ from the reference program's by a relative error of at most 0.0006.
Values may be sent and summed in bfloat16 or wider, within the bound.
A program may use at most 32 MiB of HBM per device.

```python
import math
import jax
import jax.numpy as jnp
import numpy as np
from jax import lax

D = 1024
H = 384
EXPERTS = 128
TOP = 8
TOK_DEV = 256
ITERS = 2
CAP = 32
MATS = 8
TOKENS = 262144
N_DP = 128
N_OPT = 8


def spiked(entries, key, source, target, shards_of, factor):
    def block_of(position):
        return (jnp.arange(entries.shape[position]) // (entries.shape[position] // shards_of)).reshape((-1,) + (1,) * (entries.ndim - 1 - position))

    first = jax.random.permutation(key, shards_of)[block_of(target)]
    second = (block_of(target) + shards_of // 2) % shards_of
    return jnp.where((block_of(source) == first) | (block_of(source) == second), factor * entries, entries)


def steps_of(key, extent, cuts, least, top_value):
    def one(dim, parts):
        draws = jax.random.uniform(jax.random.fold_in(jax.random.fold_in(key, 6), dim), (parts,), jnp.float32, least / len(cuts), top_value / len(cuts))
        return jnp.repeat(jnp.exp(draws), extent[dim] // parts).reshape((-1,) + (1,) * (len(extent) - dim - 1))

    loudness = one(*cuts[0])
    for cut in cuts[1:]:
        loudness = loudness * one(*cut)
    return loudness


def shared_out(own_key, own, number, rows, number_of, top, bound, slope):
    order = jax.random.permutation(own_key, number_of)
    heavy_load, common = portions_of(number_of, rows * top, bound, slope, True), portions_of(number_of, rows * top, bound, slope, False)
    places = jnp.arange(number_of)

    def named(lengths, turn):
        used = int((lengths > 0).sum())
        fixed = max(1, used // 4)
        passed = fixed + (places - fixed + turn * (used - fixed)) % max(1, number_of - fixed)
        return jnp.zeros((number_of,), jnp.int32).at[order[jnp.where(places < fixed, places, passed)]].set(jnp.asarray(lengths, jnp.int32))

    lengths = jnp.where(number % 4 == 0, named(heavy_load, number // 4), named(common, number - number // 4 - 1))
    mixed = jax.random.permutation(jax.random.fold_in(own, 3), number_of)
    source_of, taker = mixed[0:number_of // 2 * 2:2], mixed[1:number_of // 2 * 2:2]
    margin = jnp.minimum(lengths[source_of] - 1, bound - lengths[taker]) // 2
    margin = jnp.where((source_of == order[0]) | (taker == order[0]) | (lengths[taker] == 0), 0, jnp.maximum(margin, 0))
    passed = jax.random.randint(jax.random.fold_in(own, 4), (number_of // 2,), 0, 1 << 20) % (margin + 1)
    lengths = lengths.at[source_of].add(-passed).at[taker].add(passed)
    labels = jnp.searchsorted(jnp.cumsum(lengths), jnp.arange(rows * top), side="right").astype(jnp.int32)
    listing = labels.reshape(top, rows).T
    listing = listing[jax.random.permutation(jax.random.fold_in(own, 1), rows)]
    turn = jax.random.randint(jax.random.fold_in(own, 2), (rows, 1), 0, top)
    return jnp.take_along_axis(listing, (jnp.arange(top)[None, :] + turn) % top, axis=1)


def portions_of(amount, total, reach, slope, full):
    portions = [(1 << 20) // math.isqrt(rank ** slope) + 1 for rank in range(1, amount + 1)]
    largest = reach if full else min(reach, max(-(-total // amount), total * portions[0] // sum(portions)))
    least = 1 if total - largest >= amount - 1 else 0
    holding, spare = [largest] + [least] * (amount - 1), total - largest - least * (amount - 1)
    while spare > 0:
        candidates = [i for i in range(1, amount) if holding[i] < largest] or [i for i in range(1, amount) if holding[i] < reach]
        pool, remaining = sum([portions[i] for i in candidates]), spare
        for i in candidates:
            addition = min(reach - holding[i], max(1, remaining * portions[i] // pool), spare)
            holding[i] = holding[i] + addition
            spare = spare - addition
    return np.array(holding)


def noise(key, dims, scale, most, split=(), kind=jnp.bfloat16):
    result = jax.random.normal(key, dims, jnp.float32) * scale
    if len(split) > 0:
        result = steps_of(key, dims, split, -0.22, 0.18) * result
    return jnp.clip(result, min=-most, max=most).astype(kind)


def heavy_noise(rng, shape, deviation, most, split, heavy, kind=jnp.bfloat16):
    array = deviation * jax.random.normal(rng, shape, jnp.float32)
    if split:
        array = array * steps_of(rng, shape, split, -0.22, 0.18)
    return jnp.clip(spiked(array, jax.random.fold_in(rng, 3), *heavy), -most, most).astype(kind)


def setup_inputs(seed: int = 0) -> dict:
    arg_keys = jax.random.split(jax.random.key(seed), 6)
    activations = heavy_noise(arg_keys[0], (TOKENS, D), 1.0, 24.0, ((0, 1024),), (0, 1, 1024, 6.0))
    hidden_grad = noise(arg_keys[1], (TOKENS, TOP, H), 1.0, 6.0, ((0, 1024),))
    routing_keys = jax.random.split(jax.random.fold_in(arg_keys[2], 1), TOKENS // TOK_DEV)
    routing_turns = jax.random.permutation(jax.random.fold_in(arg_keys[2], 3), TOKENS // TOK_DEV)
    routing = jax.vmap(lambda own, number: shared_out(jax.random.fold_in(arg_keys[2], 2), own, number, TOK_DEV, EXPERTS, TOP, CAP, 2))(routing_keys, routing_turns).reshape((TOKENS, TOP))
    momentum = noise(arg_keys[3], (MATS, D, H), 100.0, 600.0, ((0, 8), (1, 128)), jnp.float32)
    master = noise(arg_keys[4], (MATS, D, H), 1.0, 6.0, ((0, 8), (1, 128)), jnp.float32)
    return {"activations": activations, "hidden_grad": hidden_grad, "routing": routing, "momentum": momentum, "master": master}


poly_first = 3.4445
poly_third = -4.775
poly_fifth = 2.0315
momentum_decay = 0.95
learning_rate = 0.02
weight_decay = 0.1
norm_epsilon = 1e-07

def inner_gram(first_side, second_side):
    return lax.dot_general(first_side, second_side, (((0,), (0,)), ((), ())), precision=lax.Precision.HIGHEST, preferred_element_type=jnp.float32)

def matmul_exact(first_side, second_side):
    return jnp.dot(first_side, second_side, precision=lax.Precision.HIGHEST, preferred_element_type=jnp.float32)

def newton_step(iterate, gram_now):
    polynomial = poly_third * gram_now + poly_fifth * matmul_exact(gram_now, gram_now)
    return poly_first * iterate + matmul_exact(iterate, polynomial)

def orthogonal(matrix):
    first_gram = inner_gram(matrix, matrix)
    norm_scale = lax.rsqrt(jnp.trace(first_gram) + norm_epsilon)
    iterate = matrix * norm_scale
    gram_now = first_gram * (norm_scale * norm_scale)
    for step_index in range(ITERS):
        if step_index > 0:
            gram_now = inner_gram(iterate, iterate)
        iterate = newton_step(iterate, gram_now)
    return iterate

def reference(activations, hidden_grad, routing, momentum, master):
    span = N_DP * N_OPT * CAP
    tok_count = activations.shape[0]
    positions = jnp.arange(tok_count, dtype=jnp.int32)

    def one_expert(expert):
        matched = routing == expert
        chosen = jnp.any(matched, axis=1)
        order_key = jnp.where(chosen, 0, tok_count).astype(jnp.int32) + positions
        picked = jnp.argsort(order_key)[:span]
        picked_acts = activations[picked]
        selected_grad = jnp.where(matched[picked][:, :, None], hidden_grad[picked], jnp.zeros((), hidden_grad.dtype))
        picked_grads = lax.optimization_barrier(jnp.sum(selected_grad, axis=1)).astype(hidden_grad.dtype)
        return lax.dot_general(picked_acts, picked_grads, (((0,), (0,)), ((), ())), preferred_element_type=jnp.float32)
    grads = lax.map(one_expert, jnp.arange(MATS, dtype=jnp.int32))
    momentum_out = momentum_decay * momentum + grads
    iterates = lax.map(orthogonal, momentum_out)
    update = 0.2 * math.sqrt(max(D, H)) * iterates
    master_out = (1.0 - learning_rate * weight_decay) * master - learning_rate * update
    return (momentum_out, master_out, update)
```

```python
import functools
import math

import jax
import jax.numpy as jnp
from jax import lax
from jax.experimental import pallas as pl
from jax.experimental.pallas import tpu as pltpu
from jax.sharding import PartitionSpec as P

CAP = 32
NY = 4
INNER = 4
STRIDE = 11
MESH = pl.DeviceIdType.MESH

poly_first = 3.4445
poly_third = -4.775
poly_fifth = 2.0315
momentum_decay = 0.95
learning_rate = 0.02
weight_decay = 0.1
norm_epsilon = 1e-07

f32 = jnp.float32
bf16 = jnp.bfloat16


def halves(a):
    hi = a.astype(bf16)
    return hi, (a - hi.astype(f32)).astype(bf16)


def dot(a, b):
    return jnp.dot(a, b, preferred_element_type=f32)


def dot_t(a, b):
    return lax.dot_general(a, b, (((0,), (0,)), ((), ())), preferred_element_type=f32)


def dot3(a, b):
    (a_hi, a_lo), (b_hi, b_lo) = a, b
    return dot(a_hi, b_hi) + (dot(a_hi, b_lo) + dot(a_lo, b_hi))


def one_hot(cond):
    return jnp.where(cond, 1.0, 0.0).astype(bf16)


def running_count(flags):
    width = flags.shape[1]
    lane = lax.broadcasted_iota(jnp.int32, flags.shape, 1)
    total, shift = flags, 1
    while shift < width:
        total = total + jnp.where(lane >= shift, pltpu.roll(total, shift, 1), 0)
        shift *= 2
    return total


OFFSETS = (0, 1, 7, 2, 6, 3, 5, 4)
GROUPS = ((0, 3), (3, 5), (5, 8))


def kernel(
    sizes,
    acts_hbm, hidden_hbm, names_hbm, momentum_hbm, master_hbm,
    moment_out, master_out, update_out,
    acts, hidden, names, momentum, master,
    pick, send, recv, part, near, summed, far, rows,
    load_sem, local_sem, know_four, know_eight,
    go_send, go_recv, near_send, near_recv, far_send, far_recv,
    out_send, out_recv, around_send, around_recv, side_send, side_recv,
):
    nz, n_opt = sizes
    outer = nz // INNER
    dp, opt = lax.axis_index("dp"), lax.axis_index("opt")
    z, y = dp // NY, dp % NY
    cls, place = z % INNER, z // INNER
    width = acts.shape[1]
    quarter = width // NY
    hid = hidden.shape[1]
    group = NY * n_opt

    def at(zz, yy, oo):
        return (zz * NY + yy, oo)

    def offsets(i):
        r = i * STRIDE % group
        return r // n_opt, r % n_opt

    def go_peer(i):
        dy, do = offsets(i)
        return at(z, (y + dy) % NY, (opt + do) % n_opt)

    def go_source(i):
        dy, do = offsets(i)
        return at(z, (y + NY - dy) % NY, (opt + n_opt - do) % n_opt)

    def along(dz):
        return at((z + nz + dz) % nz, y, opt)

    even = 1 - z % 2
    turn = 2 * even - (1 - even) * 2
    near_to = [along(1), along(-1), along(turn)]

    def far_to(q):
        return at((place + q) % outer * INNER + cls, y, opt)

    barrier = pltpu.get_barrier_semaphore()

    def greet(i, _):
        pl.semaphore_signal(barrier, inc=1, device_id=go_source(i), device_id_type=MESH)
        return 0

    loads = [
        pltpu.make_async_copy(source, target, load_sem.at[i])
        for i, (source, target) in enumerate(
            [
                (names_hbm, names),
                (acts_hbm, acts),
                (hidden_hbm, hidden),
                (momentum_hbm, momentum),
                (master_hbm, master),
            ]
        )
    ]
    for load in loads:
        load.start()
    lax.fori_loop(1, group, greet, 0)
    for dz in (1, -1, 2, -2, 4, -4):
        pl.semaphore_signal(barrier, inc=1, device_id=along(dz), device_id_type=MESH)

    experts, tokens, top = n_opt, acts.shape[0], names.shape[0]
    spread_shape = (tokens, tokens * top)
    spread = one_hot(
        (lax.broadcasted_iota(jnp.int32, spread_shape, 1) >> (top.bit_length() - 1))
        == lax.broadcasted_iota(jnp.int32, spread_shape, 0)
    )
    loads[0].wait()
    expert = lax.broadcasted_iota(jnp.int32, (experts, tokens), 0)
    match = jnp.zeros((experts, tokens), jnp.int32)
    for k in range(top):
        match = match + (names[k : k + 1, :] == expert).astype(jnp.int32)
    per_token = jnp.where(match > 0, running_count(match) - 1, -1)
    both = jnp.concatenate([names[...], per_token], axis=0).astype(f32).astype(bf16)
    wide = dot(both, spread)
    slot = lax.broadcasted_iota(jnp.int32, (top, tokens * top), 1) & (top - 1)
    own_slot = slot == lax.broadcasted_iota(jnp.int32, slot.shape, 0)
    name = jnp.sum(jnp.where(own_slot, wide[:top], 0.0), axis=0, keepdims=True)
    expert = lax.broadcasted_iota(jnp.int32, (experts, tokens * top), 0).astype(f32)
    flat = jnp.where(name == expert, wide[top:], -1.0)
    for e in range(experts):
        j = lax.broadcasted_iota(jnp.int32, (CAP, flat.shape[1]), 0).astype(f32)
        pick[e * CAP : (e + 1) * CAP, :] = one_hot(flat[e : e + 1, :] == j)
    loads[2].wait()
    packed_grads = dot(pick[...], hidden[...]).astype(bf16)
    j = lax.broadcasted_iota(jnp.int32, (CAP, per_token.shape[1]), 0)
    pick_acts = jnp.concatenate([one_hot(per_token[e : e + 1, :] == j) for e in range(experts)], axis=0)
    loads[1].wait()
    packed_acts = dot(pick_acts, acts[...]).astype(bf16)
    col = lax.broadcasted_iota(jnp.int32, (width, quarter), 1)
    origin = 8 * NY * (INNER * ((col >> 3) & (outer - 1)) + (col >> 6)) + (col & 7)
    row = lax.broadcasted_iota(jnp.int32, (width, quarter), 0)
    for q in range(NY):
        order = one_hot(row == origin + 8 * q)
        ordered = dot(packed_acts, order).astype(bf16)
        for e in range(experts):
            send[e, q, :, :quarter] = ordered[e * CAP : (e + 1) * CAP, :]
            send[e, q, :, quarter:] = packed_grads[e * CAP : (e + 1) * CAP, :]

    pl.semaphore_wait(barrier, group - 1 + 6)
    for dz in (4, -4):
        pl.semaphore_signal(know_four, inc=1, device_id=along(dz), device_id_type=MESH)

    def go(i):
        dy, do = offsets(i)
        return pltpu.make_async_remote_copy(
            src_ref=send.at[(opt + do) % n_opt, (y + dy) % NY],
            dst_ref=recv.at[i],
            send_sem=go_send.at[i],
            recv_sem=go_recv.at[i],
            device_id=go_peer(i),
            device_id_type=MESH,
        )

    def start_go(r, _):
        go(r).start()
        return 0

    lax.fori_loop(1, group, start_go, 0)
    own = pltpu.make_async_copy(send.at[opt, y], recv.at[0], local_sem)
    own.start()
    pl.semaphore_wait(know_four, 2)
    for dz in (8, -8):
        pl.semaphore_signal(know_eight, inc=1, device_id=along(dz), device_id_type=MESH)
    own.wait()

    def wait_go(r, _):
        go(r).wait_recv()
        return 0

    total = jnp.zeros((quarter, hid), f32)
    for chunk in range(NY):
        lax.fori_loop(max(1, chunk * n_opt), (chunk + 1) * n_opt, wait_go, 0)
        block = recv[chunk * n_opt : (chunk + 1) * n_opt].reshape(n_opt * CAP, quarter + hid)
        total = total + dot_t(block[:, :quarter], block[:, quarter:])
    part[...] = total.reshape(part.shape)

    steps = (1, INNER - 1, 2)
    nears = []
    for s in range(3):
        copy = pltpu.make_async_remote_copy(
            src_ref=part.at[(cls + steps[s]) % INNER],
            dst_ref=near.at[s],
            send_sem=near_send.at[s],
            recv_sem=near_recv.at[s],
            device_id=near_to[s],
            device_id_type=MESH,
        )
        copy.start()
        nears.append(copy)
    for copy in nears:
        copy.wait_recv()
    summed[...] = part[cls].reshape(summed.shape) + (
        near[0] + (near[1] + near[2])
    ).reshape(summed.shape)
    pl.semaphore_wait(know_eight, 2)
    fars = []
    for q in OFFSETS[:0:-1]:
        copy = pltpu.make_async_remote_copy(
            src_ref=summed.at[(place + q) % outer],
            dst_ref=far.at[q],
            send_sem=far_send.at[q],
            recv_sem=far_recv.at[q],
            device_id=far_to(q),
            device_id_type=MESH,
        )
        copy.start()
        fars.append(copy)
    loads[3].wait()
    loads[4].wait()
    grad = summed[place]
    for q, copy in zip(OFFSETS[1:], fars[::-1]):
        copy.wait_recv()
        grad = grad + far[q]
    moment = momentum_decay * momentum[...] + grad
    moment_out[...] = moment

    rows[0, 0] = moment
    outs = [None] * outer
    for i in range(outer - 1, 0, -1):
        outs[i] = pltpu.make_async_remote_copy(
            src_ref=rows.at[0, 0],
            dst_ref=rows.at[0, i],
            send_sem=out_send.at[i],
            recv_sem=out_recv.at[i],
            device_id=far_to(OFFSETS[i]),
            device_id_type=MESH,
        )
        outs[i].start()
    arounds, sides = {}, {}

    def to_sides(s, g):
        begin, end = GROUPS[g]
        for d in range(1, NY):
            slot = d * INNER + s
            sides[slot, g] = pltpu.make_async_remote_copy(
                src_ref=rows.at[s, begin:end],
                dst_ref=rows.at[slot, begin:end],
                send_sem=side_send.at[slot, g],
                recv_sem=side_recv.at[slot, g],
                device_id=at(z, (y + d) % NY, opt),
                device_id_type=MESH,
            )
            sides[slot, g].start()

    def from_places(g):
        begin, end = GROUPS[g]
        for i in range(max(begin, 1), end):
            outs[i].wait_recv()
        for s in range(1, INNER):
            arounds[s, g] = pltpu.make_async_remote_copy(
                src_ref=rows.at[0, begin:end],
                dst_ref=rows.at[s, begin:end],
                send_sem=around_send.at[s, g],
                recv_sem=around_recv.at[s, g],
                device_id=near_to[s - 1],
                device_id_type=MESH,
            )
            arounds[s, g].start()
        to_sides(0, g)

    def from_classes(g):
        for s in range(1, INNER):
            arounds[s, g].wait_recv()
            to_sides(s, g)

    last = len(GROUPS)
    for g in range(last + 1):
        if g < last:
            from_places(g)
        if g > 0:
            from_classes(g - 1)
    gram_hi = jnp.zeros((hid, hid), f32)
    gram_lo = jnp.zeros((hid, hid), f32)
    for g, (begin, end) in enumerate(GROUPS):
        for slot in range(INNER, NY * INNER):
            sides[slot, g].wait_recv()
        hi, lo = halves(rows[:, begin:end].reshape(NY * INNER * (end - begin) * 8, hid))
        gram_hi, gram_lo = gram_hi + dot_t(hi, hi), gram_lo + dot_t(hi, lo)

    gram = gram_hi + (gram_lo + gram_lo.T)
    eye = lax.broadcasted_iota(jnp.int32, gram.shape, 0) == lax.broadcasted_iota(jnp.int32, gram.shape, 1)
    scale = lax.rsqrt(jnp.sum(jnp.where(eye, gram, 0.0)) + norm_epsilon)
    one = jnp.where(eye, poly_first, 0.0)
    gram = gram * (scale * scale)
    gram_parts = halves(gram)
    first = one + (poly_third * gram + poly_fifth * dot3(gram_parts, gram_parts))
    first_parts = halves(first)
    later = dot3(first_parts, halves(dot3(gram_parts, first_parts)))
    later_parts = halves(later)
    second = one + (poly_third * later + poly_fifth * dot3(later_parts, later_parts))
    iterate = dot3(halves(dot3(halves(moment * scale), first_parts)), halves(second))
    update = 0.2 * math.sqrt(max(width, hid)) * iterate
    update_out[...] = update
    master_out[...] = (1.0 - learning_rate * weight_decay) * master[...] - learning_rate * update

    def wait_sent(i, _):
        go(i).wait_send()
        return 0

    lax.fori_loop(1, group, wait_sent, 0)
    for copy in nears + fars + outs[1:] + list(arounds.values()) + list(sides.values()):
        copy.wait_send()


def per_device(activations, hidden_grad, routing, momentum, master):
    n_opt = lax.axis_size("opt")
    nz = lax.axis_size("dp") // NY
    outer = nz // INNER
    tokens, width = activations.shape
    top, hid = hidden_grad.shape[1:]
    quarter = width // NY
    group = NY * n_opt
    dma = pltpu.SemaphoreType.DMA
    shape = jax.ShapeDtypeStruct(momentum.shape[1:], f32)
    vmem = pl.BlockSpec(memory_space=pltpu.VMEM)
    outs = pl.pallas_call(
        functools.partial(kernel, (nz, n_opt)),
        out_shape=(shape, shape, shape),
        in_specs=[pl.BlockSpec(memory_space=pltpu.HBM)] * 5,
        out_specs=(vmem, vmem, vmem),
        scratch_shapes=[
            pltpu.VMEM((tokens, width), bf16),
            pltpu.VMEM((tokens * top, hid), bf16),
            pltpu.VMEM((top, tokens), jnp.int32),
            pltpu.VMEM(shape.shape, f32),
            pltpu.VMEM(shape.shape, f32),
            pltpu.VMEM((n_opt * CAP, tokens * top), bf16),
            pltpu.VMEM((n_opt, NY, CAP, quarter + hid), bf16),
            pltpu.VMEM((group, CAP, quarter + hid), bf16),
            pltpu.VMEM((INNER, outer * 8, hid), f32),
            pltpu.VMEM((3, outer * 8, hid), f32),
            pltpu.VMEM((outer, 8, hid), f32),
            pltpu.VMEM((outer, 8, hid), f32),
            pltpu.VMEM((NY * INNER, outer, 8, hid), f32),
            dma((5,)),
            dma,
            pltpu.SemaphoreType.REGULAR,
            pltpu.SemaphoreType.REGULAR,
            dma((group,)), dma((group,)),
            dma((3,)), dma((3,)),
            dma((outer,)), dma((outer,)),
            dma((outer,)), dma((outer,)),
            dma((INNER, len(GROUPS))), dma((INNER, len(GROUPS))),
            dma((NY * INNER, len(GROUPS))), dma((NY * INNER, len(GROUPS))),
        ],
        compiler_params=pltpu.CompilerParams(
            collective_id=0, has_side_effects=True, vmem_limit_bytes=60 * 1024 * 1024
        ),
    )(
        activations,
        hidden_grad.reshape(tokens * top, hid),
        routing.T,
        momentum[0],
        master[0],
    )
    return tuple(out[None] for out in outs)


def solution(mesh):
    placed = (
        P(("dp", "opt"), None),
        P(("dp", "opt"), None, None),
        P(("dp", "opt"), None),
        P("opt", "dp", None),
        P("opt", "dp", None),
    )
    return jax.shard_map(
        per_device,
        mesh=mesh,
        in_specs=placed,
        out_specs=(P("opt", "dp", None), P("opt", "dp", None), P("opt", "dp", None)),
        check_vma=False,
    )
```

```python
import functools
import math

import jax
import jax.numpy as jnp
from jax import lax
from jax.experimental import pallas as pl
from jax.experimental.pallas import tpu as pltpu
from jax.sharding import PartitionSpec as P

CAP = 32
NY = 4
INNER = 4
STRIDE = 5
MESH = pl.DeviceIdType.MESH

poly_first = 3.4445
poly_third = -4.775
poly_fifth = 2.0315
momentum_decay = 0.95
learning_rate = 0.02
weight_decay = 0.1
norm_epsilon = 1e-07

f32 = jnp.float32
bf16 = jnp.bfloat16


def halves(a):
    hi = a.astype(bf16)
    return hi, (a - hi.astype(f32)).astype(bf16)


def dot(a, b):
    return jnp.dot(a, b, preferred_element_type=f32)


def dot_t(a, b):
    return lax.dot_general(a, b, (((0,), (0,)), ((), ())), preferred_element_type=f32)


def dot3(a, b):
    (a_hi, a_lo), (b_hi, b_lo) = a, b
    return dot(a_hi, b_hi) + (dot(a_hi, b_lo) + dot(a_lo, b_hi))


def one_hot(cond):
    return jnp.where(cond, 1.0, 0.0).astype(bf16)


def step_of(exponent, mantissa):
    return mantissa * (jnp.exp2(exponent - 14.0) * (1 / 32767))


def coded(block):
    peak = jnp.maximum(jnp.max(jnp.abs(block), keepdims=True), 1e-30)
    exponent = jnp.floor(jnp.log(peak) * (1 / math.log(2)) + 0.001) + 1.0
    mantissa = jnp.floor(peak * jnp.exp2(14.0 - exponent)) + 2.0
    steps = jnp.round(block * (1.0 / step_of(exponent, mantissa)))
    parts = [steps[:, c : c + 128] for c in range(0, block.shape[1], 128)]
    first_half = lax.broadcasted_iota(jnp.int32, (8, 128), 0) < 4
    parts.append(jnp.where(first_half, exponent, mantissa))
    return jnp.concatenate(parts, axis=0).astype(jnp.int32).astype(jnp.int16)


def decoded(blocks):
    parts = blocks.astype(jnp.int32).astype(f32).reshape(-1, 4, 8, 128)
    step = step_of(parts[:, 3, 0:1], parts[:, 3, 4:5])
    return jnp.concatenate([(parts[:, c] * step).reshape(-1, 128) for c in range(3)], axis=1)


def running_count(flags):
    width = flags.shape[1]
    lane = lax.broadcasted_iota(jnp.int32, flags.shape, 1)
    total, shift = flags, 1
    while shift < width:
        total = total + jnp.where(lane >= shift, pltpu.roll(total, shift, 1), 0)
        shift *= 2
    return total


OFFSETS = (0, 1, 7, 2, 6, 3, 5, 4)
GROUPS = ((0, 3), (3, 5), (5, 8))


def kernel(
    sizes,
    acts_hbm, hidden_hbm, names_hbm, momentum_hbm,
    result,
    acts, hidden, names, momentum,
    pick, send, recv, part, near, summed, far, rows,
    load_sem, local_sem, know_four, know_eight,
    go_send, go_recv, near_send, near_recv, far_send, far_recv,
    out_send, out_recv, around_send, around_recv, side_send, side_recv,
):
    nz, n_opt = sizes
    outer = nz // INNER
    dp, opt = lax.axis_index("dp"), lax.axis_index("opt")
    z, y = dp // NY, dp % NY
    cls, place = z % INNER, z // INNER
    width = acts.shape[1]
    quarter = width // NY
    hid = hidden.shape[1]
    group = NY * n_opt

    def at(zz, yy, oo):
        return (zz * NY + yy, oo)

    def offsets(i):
        r = i * STRIDE % group
        return r // n_opt, r % n_opt

    def go_peer(i):
        dy, do = offsets(i)
        return at(z, (y + dy) % NY, (opt + do) % n_opt)

    def go_source(i):
        dy, do = offsets(i)
        return at(z, (y + NY - dy) % NY, (opt + n_opt - do) % n_opt)

    def along(dz):
        return at((z + nz + dz) % nz, y, opt)

    even = 1 - z % 2
    turn = 2 * even - (1 - even) * 2
    near_to = [along(1), along(-1), along(turn)]

    def far_to(q):
        return at((place + q) % outer * INNER + cls, y, opt)

    barrier = pltpu.get_barrier_semaphore()

    def greet(i, _):
        pl.semaphore_signal(barrier, inc=1, device_id=go_source(i), device_id_type=MESH)
        return 0

    loads = [
        pltpu.make_async_copy(source, target, load_sem.at[i])
        for i, (source, target) in enumerate(
            [
                (names_hbm, names),
                (acts_hbm, acts),
                (hidden_hbm, hidden),
                (momentum_hbm, momentum),
            ]
        )
    ]
    loads[0].start()
    for dz in (4, -4, 2, -2, 1, -1):
        pl.semaphore_signal(barrier, inc=1, device_id=along(dz), device_id_type=MESH)
    for load in loads[1:]:
        load.start()
    lax.fori_loop(1, group, greet, 0)

    experts, tokens, top = n_opt, acts.shape[0], names.shape[0]
    spread_shape = (tokens, tokens * top)
    spread = one_hot(
        (lax.broadcasted_iota(jnp.int32, spread_shape, 1) >> (top.bit_length() - 1))
        == lax.broadcasted_iota(jnp.int32, spread_shape, 0)
    )
    loads[0].wait()
    expert = lax.broadcasted_iota(jnp.int32, (experts, tokens), 0)
    match = jnp.zeros((experts, tokens), jnp.int32)
    for k in range(top):
        match = match + (names[k : k + 1, :] == expert).astype(jnp.int32)
    per_token = jnp.where(match > 0, running_count(match) - 1, -1)
    both = jnp.concatenate([names[...], per_token], axis=0).astype(f32).astype(bf16)
    wide = dot(both, spread)
    slot = lax.broadcasted_iota(jnp.int32, (top, tokens * top), 1) & (top - 1)
    own_slot = slot == lax.broadcasted_iota(jnp.int32, slot.shape, 0)
    name = jnp.sum(jnp.where(own_slot, wide[:top], 0.0), axis=0, keepdims=True)
    expert = lax.broadcasted_iota(jnp.int32, (experts, tokens * top), 0).astype(f32)
    flat = jnp.where(name == expert, wide[top:], -1.0)
    for e in range(experts):
        j = lax.broadcasted_iota(jnp.int32, (CAP, flat.shape[1]), 0).astype(f32)
        pick[e * CAP : (e + 1) * CAP, :] = one_hot(flat[e : e + 1, :] == j)
    loads[2].wait()
    packed_grads = dot(pick[...], hidden[...]).astype(bf16)
    j = lax.broadcasted_iota(jnp.int32, (CAP, per_token.shape[1]), 0)
    pick_acts = jnp.concatenate([one_hot(per_token[e : e + 1, :] == j) for e in range(experts)], axis=0)
    loads[1].wait()
    packed_acts = dot(pick_acts, acts[...]).astype(bf16)
    col = lax.broadcasted_iota(jnp.int32, (width, quarter), 1)
    origin = 8 * NY * (INNER * ((col >> 3) & (outer - 1)) + (col >> 6)) + (col & 7)
    row = lax.broadcasted_iota(jnp.int32, (width, quarter), 0)
    for q in range(NY):
        order = one_hot(row == origin + 8 * q)
        ordered = dot(packed_acts, order).astype(bf16)
        for e in range(experts):
            send[e, q, :, :quarter] = ordered[e * CAP : (e + 1) * CAP, :]
            send[e, q, :, quarter:] = packed_grads[e * CAP : (e + 1) * CAP, :]

    pl.semaphore_wait(barrier, group - 1 + 6)
    for dz in (4, -4):
        pl.semaphore_signal(know_four, inc=1, device_id=along(dz), device_id_type=MESH)

    def go(i):
        dy, do = offsets(i)
        return pltpu.make_async_remote_copy(
            src_ref=send.at[(opt + do) % n_opt, (y + dy) % NY],
            dst_ref=recv.at[i],
            send_sem=go_send.at[i],
            recv_sem=go_recv.at[i],
            device_id=go_peer(i),
            device_id_type=MESH,
        )

    def start_go(r, _):
        go(r).start()
        return 0

    lax.fori_loop(1, group, start_go, 0)
    own = pltpu.make_async_copy(send.at[opt, y], recv.at[0], local_sem)
    own.start()
    pl.semaphore_wait(know_four, 2)
    for dz in (8, -8):
        pl.semaphore_signal(know_eight, inc=1, device_id=along(dz), device_id_type=MESH)
    own.wait()

    def wait_go(r, _):
        go(r).wait_recv()
        return 0

    total = jnp.zeros((quarter, hid), f32)
    for chunk in range(NY):
        lax.fori_loop(max(1, chunk * n_opt), (chunk + 1) * n_opt, wait_go, 0)
        block = recv[chunk * n_opt : (chunk + 1) * n_opt].reshape(n_opt * CAP, quarter + hid)
        total = total + dot_t(block[:, :quarter], block[:, quarter:])
    part[...] = total.reshape(part.shape)

    steps = (1, INNER - 1, 2)
    nears = []
    for s in range(3):
        copy = pltpu.make_async_remote_copy(
            src_ref=part.at[(cls + steps[s]) % INNER],
            dst_ref=near.at[s],
            send_sem=near_send.at[s],
            recv_sem=near_recv.at[s],
            device_id=near_to[s],
            device_id_type=MESH,
        )
        copy.start()
        nears.append(copy)
    for copy in nears:
        copy.wait_recv()
    summed[...] = part[cls].reshape(summed.shape) + (
        near[0] + (near[1] + near[2])
    ).reshape(summed.shape)
    pl.semaphore_wait(know_eight, 2)
    fars = []
    for q in OFFSETS[:0:-1]:
        copy = pltpu.make_async_remote_copy(
            src_ref=summed.at[(place + q) % outer],
            dst_ref=far.at[q],
            send_sem=far_send.at[q],
            recv_sem=far_recv.at[q],
            device_id=far_to(q),
            device_id_type=MESH,
        )
        copy.start()
        fars.append(copy)
    loads[3].wait()
    grad = summed[place]
    for q, copy in zip(OFFSETS[1:], fars[::-1]):
        copy.wait_recv()
        grad = grad + far[q]
    moment = momentum_decay * momentum[...] + grad
    result[0] = moment

    rows[0, 0] = coded(moment)
    outs = [None] * outer
    for i in range(outer - 1, 0, -1):
        outs[i] = pltpu.make_async_remote_copy(
            src_ref=rows.at[0, 0],
            dst_ref=rows.at[0, i],
            send_sem=out_send.at[i],
            recv_sem=out_recv.at[i],
            device_id=far_to(OFFSETS[i]),
            device_id_type=MESH,
        )
        outs[i].start()
    arounds, sides = {}, {}

    def to_sides(s, g):
        begin, end = GROUPS[g]
        for d in range(1, NY):
            slot = d * INNER + s
            sides[slot, g] = pltpu.make_async_remote_copy(
                src_ref=rows.at[s, begin:end],
                dst_ref=rows.at[slot, begin:end],
                send_sem=side_send.at[slot, g],
                recv_sem=side_recv.at[slot, g],
                device_id=at(z, (y + d) % NY, opt),
                device_id_type=MESH,
            )
            sides[slot, g].start()

    def from_places(g):
        begin, end = GROUPS[g]
        for i in range(max(begin, 1), end):
            outs[i].wait_recv()
        for s in range(1, INNER):
            arounds[s, g] = pltpu.make_async_remote_copy(
                src_ref=rows.at[0, begin:end],
                dst_ref=rows.at[s, begin:end],
                send_sem=around_send.at[s, g],
                recv_sem=around_recv.at[s, g],
                device_id=near_to[s - 1],
                device_id_type=MESH,
            )
            arounds[s, g].start()
        to_sides(0, g)

    def from_classes(g):
        for s in range(1, INNER):
            arounds[s, g].wait_recv()
            to_sides(s, g)

    last = len(GROUPS)
    for g in range(last + 1):
        if g < last:
            from_places(g)
        if g > 0:
            from_classes(g - 1)
    gram_hi = jnp.zeros((hid, hid), f32)
    gram_lo = jnp.zeros((hid, hid), f32)
    for g, (begin, end) in enumerate(GROUPS):
        for slot in range(INNER, NY * INNER):
            sides[slot, g].wait_recv()
        hi, lo = halves(decoded(rows[:, begin:end]))
        gram_hi, gram_lo = gram_hi + dot_t(hi, hi), gram_lo + dot_t(hi, lo)

    gram = gram_hi + (gram_lo + gram_lo.T)
    eye = lax.broadcasted_iota(jnp.int32, gram.shape, 0) == lax.broadcasted_iota(jnp.int32, gram.shape, 1)
    scale = lax.rsqrt(jnp.sum(jnp.where(eye, gram, 0.0)) + norm_epsilon)
    one = jnp.where(eye, poly_first, 0.0)
    gram = gram * (scale * scale)
    gram_parts = halves(gram)
    first = one + (poly_third * gram + poly_fifth * dot3(gram_parts, gram_parts))
    first_parts = halves(first)
    later = dot3(first_parts, halves(dot3(gram_parts, first_parts)))
    later_parts = halves(later)
    second = one + (poly_third * later + poly_fifth * dot3(later_parts, later_parts))
    result[1] = dot3(halves(dot3(halves(moment * scale), first_parts)), halves(second))

    def wait_sent(i, _):
        go(i).wait_send()
        return 0

    lax.fori_loop(1, group, wait_sent, 0)
    for copy in nears + fars + outs[1:] + list(arounds.values()) + list(sides.values()):
        copy.wait_send()


def per_device(activations, hidden_grad, routing, momentum, master):
    n_opt = lax.axis_size("opt")
    nz = lax.axis_size("dp") // NY
    outer = nz // INNER
    tokens, width = activations.shape
    top, hid = hidden_grad.shape[1:]
    quarter = width // NY
    group = NY * n_opt
    dma = pltpu.SemaphoreType.DMA
    shape = jax.ShapeDtypeStruct(momentum.shape[1:], f32)
    vmem = pl.BlockSpec(memory_space=pltpu.VMEM)
    result = pl.pallas_call(
        functools.partial(kernel, (nz, n_opt)),
        out_shape=jax.ShapeDtypeStruct((2, *shape.shape), f32),
        in_specs=[pl.BlockSpec(memory_space=pltpu.HBM)] * 4,
        out_specs=vmem,
        scratch_shapes=[
            pltpu.VMEM((tokens, width), bf16),
            pltpu.VMEM((tokens * top, hid), bf16),
            pltpu.VMEM((top, tokens), jnp.int32),
            pltpu.VMEM(shape.shape, f32),
            pltpu.VMEM((n_opt * CAP, tokens * top), bf16),
            pltpu.VMEM((n_opt, NY, CAP, quarter + hid), bf16),
            pltpu.VMEM((group, CAP, quarter + hid), bf16),
            pltpu.VMEM((INNER, outer * 8, hid), f32),
            pltpu.VMEM((3, outer * 8, hid), f32),
            pltpu.VMEM((outer, 8, hid), f32),
            pltpu.VMEM((outer, 8, hid), f32),
            pltpu.VMEM((NY * INNER, outer, 32, 128), jnp.int16),
            dma((4,)),
            dma,
            pltpu.SemaphoreType.REGULAR,
            pltpu.SemaphoreType.REGULAR,
            dma((group,)), dma((group,)),
            dma((3,)), dma((3,)),
            dma((outer,)), dma((outer,)),
            dma((outer,)), dma((outer,)),
            dma((INNER, len(GROUPS))), dma((INNER, len(GROUPS))),
            dma((NY * INNER, len(GROUPS))), dma((NY * INNER, len(GROUPS))),
        ],
        compiler_params=pltpu.CompilerParams(
            collective_id=0, has_side_effects=True, vmem_limit_bytes=60 * 1024 * 1024
        ),
    )(
        activations,
        hidden_grad.reshape(tokens * top, hid),
        routing.T,
        momentum[0],
    )
    new_moment, iterate = result[:1], result[1:]
    update = 0.2 * math.sqrt(max(width, hid)) * iterate
    master_out = (1.0 - learning_rate * weight_decay) * master - learning_rate * update
    return (new_moment, master_out, update)


def solution(mesh):
    placed = (
        P(("dp", "opt"), None),
        P(("dp", "opt"), None, None),
        P(("dp", "opt"), None),
        P("opt", "dp", None),
        P("opt", "dp", None),
    )
    return jax.shard_map(
        per_device,
        mesh=mesh,
        in_specs=placed,
        out_specs=(P("opt", "dp", None), P("opt", "dp", None), P("opt", "dp", None)),
        check_vma=False,
    )
```

```python
import functools
import math

import jax
import jax.numpy as jnp
from jax import lax
from jax.experimental import pallas as pl
from jax.experimental.pallas import tpu as pltpu
from jax.sharding import PartitionSpec as P

CAP = 32
NY = 4
INNER = 4
STRIDE = 5
MESH = pl.DeviceIdType.MESH

poly_first = 3.4445
poly_third = -4.775
poly_fifth = 2.0315
momentum_decay = 0.95
learning_rate = 0.02
weight_decay = 0.1
norm_epsilon = 1e-07

f32 = jnp.float32
bf16 = jnp.bfloat16


def halves(a):
    hi = a.astype(bf16)
    return hi, (a - hi.astype(f32)).astype(bf16)


def dot(a, b):
    return jnp.dot(a, b, preferred_element_type=f32)


def dot_t(a, b):
    return lax.dot_general(a, b, (((0,), (0,)), ((), ())), preferred_element_type=f32)


def dot3(a, b):
    (a_hi, a_lo), (b_hi, b_lo) = a, b
    return dot(a_hi, b_hi) + (dot(a_hi, b_lo) + dot(a_lo, b_hi))


def one_hot(cond):
    return jnp.where(cond, 1.0, 0.0).astype(bf16)


def step_of(exponent, mantissa):
    return mantissa * (jnp.exp2(exponent - 14.0) * (1 / 32767))


def coded(block):
    peak = jnp.maximum(jnp.max(jnp.abs(block), keepdims=True), 1e-30)
    exponent = jnp.floor(jnp.log(peak) * (1 / math.log(2)) + 0.001) + 1.0
    mantissa = jnp.floor(peak * jnp.exp2(14.0 - exponent)) + 2.0
    steps = jnp.round(block * (1.0 / step_of(exponent, mantissa)))
    parts = [steps[:, c : c + 128] for c in range(0, block.shape[1], 128)]
    first_half = lax.broadcasted_iota(jnp.int32, (8, 128), 0) < 4
    parts.append(jnp.where(first_half, exponent, mantissa))
    return jnp.concatenate(parts, axis=0).astype(jnp.int32).astype(jnp.int16)


def decoded(blocks):
    parts = blocks.astype(jnp.int32).astype(f32).reshape(-1, 4, 8, 128)
    step = step_of(parts[:, 3, 0:1], parts[:, 3, 4:5])
    return jnp.concatenate([(parts[:, c] * step).reshape(-1, 128) for c in range(3)], axis=1)


def running_count(flags):
    width = flags.shape[1]
    lane = lax.broadcasted_iota(jnp.int32, flags.shape, 1)
    total, shift = flags, 1
    while shift < width:
        total = total + jnp.where(lane >= shift, pltpu.roll(total, shift, 1), 0)
        shift *= 2
    return total


OFFSETS = (0, 1, 7, 2, 6, 3, 5, 4)
GROUPS = ((0, 3), (3, 5), (5, 8))


def kernel(
    sizes,
    acts_hbm, hidden_hbm, names_hbm, momentum_hbm,
    result,
    acts, hidden, names, momentum,
    pick, send, recv, part, near, summed, far, rows,
    load_sem, local_sem, know_four, know_eight,
    go_send, go_recv, near_send, near_recv, far_send, far_recv,
    out_send, out_recv, around_send, around_recv, side_send, side_recv,
):
    nz, n_opt = sizes
    outer = nz // INNER
    dp, opt = lax.axis_index("dp"), lax.axis_index("opt")
    z, y = dp // NY, dp % NY
    cls, place = z % INNER, z // INNER
    width = acts.shape[1]
    quarter = width // NY
    hid = hidden.shape[1]
    group = NY * n_opt

    def at(zz, yy, oo):
        return (zz * NY + yy, oo)

    def offsets(i):
        r = i * STRIDE % group
        return r // n_opt, r % n_opt

    def go_peer(i):
        dy, do = offsets(i)
        return at(z, (y + dy) % NY, (opt + do) % n_opt)

    def along(dz):
        return at((z + nz + dz) % nz, y, opt)

    even = 1 - z % 2
    turn = 2 * even - (1 - even) * 2
    near_to = [along(1), along(-1), along(turn)]

    def far_to(q):
        return at((place + q) % outer * INNER + cls, y, opt)

    barrier = pltpu.get_barrier_semaphore()

    def greet(i, _):
        target = at(z, (y + NY // 2 + i // n_opt) % NY, (opt + n_opt // 2 + i % n_opt) % n_opt)
        pl.semaphore_signal(barrier, inc=1, device_id=target, device_id_type=MESH)
        return 0

    loads = [
        pltpu.make_async_copy(source, target, load_sem.at[i])
        for i, (source, target) in enumerate(
            [
                (names_hbm, names),
                (acts_hbm, acts),
                (hidden_hbm, hidden),
                (momentum_hbm, momentum),
            ]
        )
    ]
    own = NY // 2 * n_opt + n_opt // 2
    loads[0].start()
    for dz in (4, -4):
        pl.semaphore_signal(barrier, inc=1, device_id=along(dz), device_id_type=MESH)
    lax.fori_loop(0, own, greet, 0)
    for load in loads[1:]:
        load.start()
    lax.fori_loop(own + 1, group, greet, 0)
    for dz in (2, -2, 1, -1):
        pl.semaphore_signal(barrier, inc=1, device_id=along(dz), device_id_type=MESH)

    experts, tokens, top = n_opt, acts.shape[0], names.shape[0]
    spread_shape = (tokens, tokens * top)
    spread = one_hot(
        (lax.broadcasted_iota(jnp.int32, spread_shape, 1) >> (top.bit_length() - 1))
        == lax.broadcasted_iota(jnp.int32, spread_shape, 0)
    )
    loads[0].wait()
    expert = lax.broadcasted_iota(jnp.int32, (experts, tokens), 0)
    match = jnp.zeros((experts, tokens), jnp.int32)
    for k in range(top):
        match = match + (names[k : k + 1, :] == expert).astype(jnp.int32)
    per_token = jnp.where(match > 0, running_count(match) - 1, -1)
    both = jnp.concatenate([names[...], per_token], axis=0).astype(f32).astype(bf16)
    wide = dot(both, spread)
    slot = lax.broadcasted_iota(jnp.int32, (top, tokens * top), 1) & (top - 1)
    own_slot = slot == lax.broadcasted_iota(jnp.int32, slot.shape, 0)
    name = jnp.sum(jnp.where(own_slot, wide[:top], 0.0), axis=0, keepdims=True)
    expert = lax.broadcasted_iota(jnp.int32, (experts, tokens * top), 0).astype(f32)
    flat = jnp.where(name == expert, wide[top:], -1.0)
    for e in range(experts):
        j = lax.broadcasted_iota(jnp.int32, (CAP, flat.shape[1]), 0).astype(f32)
        pick[e * CAP : (e + 1) * CAP, :] = one_hot(flat[e : e + 1, :] == j)
    loads[2].wait()
    packed_grads = dot(pick[...], hidden[...]).astype(bf16)
    j = lax.broadcasted_iota(jnp.int32, (CAP, per_token.shape[1]), 0)
    pick_acts = jnp.concatenate([one_hot(per_token[e : e + 1, :] == j) for e in range(experts)], axis=0)
    loads[1].wait()
    packed_acts = dot(pick_acts, acts[...]).astype(bf16)
    parts = []
    row = lax.broadcasted_iota(jnp.int32, (quarter, quarter), 0)
    lane = lax.broadcasted_iota(jnp.int32, (quarter, quarter), 1)
    in_class = (((lane >> 3) & 1) * INNER + ((lane >> 4) & 3)) * (8 * NY) + (lane & 7)
    for i in range(NY):
        origin = in_class + ((((lane >> 6) + (NY - i)) & (NY - 1)) << 3)
        ordered = dot(packed_acts[:, i * quarter : (i + 1) * quarter], one_hot(row == origin))
        parts.append(ordered)
    low = (lax.broadcasted_iota(jnp.int32, (n_opt * CAP, 128), 1) & 64) == 0
    for q in range(NY):
        for half in range(2):
            lanes = slice(128 * half, 128 * half + 128)
            pieces = [parts[(2 * half + k + NY - q) % NY][:, lanes] for k in range(2)]
            piece = jnp.where(low, pieces[0], pieces[1]).astype(bf16)
            for e in range(experts):
                send[e, q, :, lanes] = piece[e * CAP : (e + 1) * CAP, :]
        for e in range(experts):
            send[e, q, :, quarter:] = packed_grads[e * CAP : (e + 1) * CAP, :]

    pl.semaphore_wait(barrier, group - 1 + 6)
    def go(i):
        dy, do = offsets(i)
        return pltpu.make_async_remote_copy(
            src_ref=send.at[(opt + do) % n_opt, (y + dy) % NY],
            dst_ref=recv.at[i],
            send_sem=go_send.at[i],
            recv_sem=go_recv.at[i],
            device_id=go_peer(i),
            device_id_type=MESH,
        )

    def start_go(r, _):
        go(r).start()
        return 0

    lax.fori_loop(1, group, start_go, 0)
    for dz in (4, -4):
        pl.semaphore_signal(know_four, inc=1, device_id=along(dz), device_id_type=MESH)
    own = pltpu.make_async_copy(send.at[opt, y], recv.at[0], local_sem)
    own.start()
    pl.semaphore_wait(know_four, 2)
    for dz in (8, -8):
        pl.semaphore_signal(know_eight, inc=1, device_id=along(dz), device_id_type=MESH)
    own.wait()

    def wait_go(r, _):
        go(r).wait_recv()
        return 0

    total = jnp.zeros((quarter, hid), f32)
    for begin, end in ((0, 8), (8, 16), (16, 24), (24, 28), (28, 32)):
        lax.fori_loop(max(1, begin), end, wait_go, 0)
        block = recv[begin:end].reshape((end - begin) * CAP, quarter + hid)
        total = total + dot_t(block[:, :quarter], block[:, quarter:])
    for p in range(NY):
        for c in range(INNER):
            rows_at = p * 64 + c * 16
            pair = pl.ds(2 * ((p + NY - y) % NY), 2)
            part[c, pair] = total[rows_at : rows_at + 16].reshape(2, 8, hid)

    steps = (1, INNER - 1, 2)
    nears = []
    for s in range(3):
        copy = pltpu.make_async_remote_copy(
            src_ref=part.at[(cls + steps[s]) % INNER],
            dst_ref=near.at[s],
            send_sem=near_send.at[s],
            recv_sem=near_recv.at[s],
            device_id=near_to[s],
            device_id_type=MESH,
        )
        copy.start()
        nears.append(copy)
    for copy in nears:
        copy.wait_recv()
    summed[...] = part[cls] + (near[0] + (near[1] + near[2]))
    pl.semaphore_wait(know_eight, 2)
    fars = []
    for q in OFFSETS[:0:-1]:
        copy = pltpu.make_async_remote_copy(
            src_ref=summed.at[(place + q) % outer],
            dst_ref=far.at[q],
            send_sem=far_send.at[q],
            recv_sem=far_recv.at[q],
            device_id=far_to(q),
            device_id_type=MESH,
        )
        copy.start()
        fars.append(copy)
    loads[3].wait()
    grad = summed[place]
    for q, copy in zip(OFFSETS[1:], fars[::-1]):
        copy.wait_recv()
        grad = grad + far[q]
    moment = momentum_decay * momentum[...] + grad
    result[0] = moment

    rows[0, 0] = coded(moment)
    outs = [None] * outer
    for i in range(outer - 1, 0, -1):
        outs[i] = pltpu.make_async_remote_copy(
            src_ref=rows.at[0, 0],
            dst_ref=rows.at[0, i],
            send_sem=out_send.at[i],
            recv_sem=out_recv.at[i],
            device_id=far_to(OFFSETS[i]),
            device_id_type=MESH,
        )
        outs[i].start()
    arounds, sides = {}, {}

    def to_sides(s, g):
        begin, end = GROUPS[g]
        for d in range(1, NY):
            slot = d * INNER + s
            sides[slot, g] = pltpu.make_async_remote_copy(
                src_ref=rows.at[s, begin:end],
                dst_ref=rows.at[slot, begin:end],
                send_sem=side_send.at[slot, g],
                recv_sem=side_recv.at[slot, g],
                device_id=at(z, (y + d) % NY, opt),
                device_id_type=MESH,
            )
            sides[slot, g].start()

    def from_places(g):
        begin, end = GROUPS[g]
        for i in range(max(begin, 1), end):
            outs[i].wait_recv()
        for s in range(1, INNER):
            arounds[s, g] = pltpu.make_async_remote_copy(
                src_ref=rows.at[0, begin:end],
                dst_ref=rows.at[s, begin:end],
                send_sem=around_send.at[s, g],
                recv_sem=around_recv.at[s, g],
                device_id=near_to[s - 1],
                device_id_type=MESH,
            )
            arounds[s, g].start()
        to_sides(0, g)

    def from_classes(g):
        for s in range(1, INNER):
            arounds[s, g].wait_recv()
            to_sides(s, g)

    last = len(GROUPS)
    for g in range(last + 1):
        if g < last:
            from_places(g)
        if g > 0:
            from_classes(g - 1)
    gram_hi = jnp.zeros((hid, hid), f32)
    gram_lo = jnp.zeros((hid, hid), f32)
    for g, (begin, end) in enumerate(GROUPS):
        for slot in range(INNER, NY * INNER):
            sides[slot, g].wait_recv()
        hi, lo = halves(decoded(rows[:, begin:end]))
        gram_hi, gram_lo = gram_hi + dot_t(hi, hi), gram_lo + dot_t(hi, lo)

    gram = gram_hi + (gram_lo + gram_lo.T)
    eye = lax.broadcasted_iota(jnp.int32, gram.shape, 0) == lax.broadcasted_iota(jnp.int32, gram.shape, 1)
    scale = lax.rsqrt(jnp.sum(jnp.where(eye, gram, 0.0)) + norm_epsilon)
    one = jnp.where(eye, poly_first, 0.0)
    gram = gram * (scale * scale)
    gram_parts = halves(gram)
    first = one + (poly_third * gram + poly_fifth * dot3(gram_parts, gram_parts))
    first_parts = halves(first)
    later = dot3(first_parts, halves(dot3(gram_parts, first_parts)))
    later_parts = halves(later)
    second = one + (poly_third * later + poly_fifth * dot3(later_parts, later_parts))
    result[1] = dot3(halves(dot3(halves(moment * scale), first_parts)), halves(second))

    def wait_sent(i, _):
        go(i).wait_send()
        return 0

    lax.fori_loop(1, group, wait_sent, 0)
    for copy in nears + fars + outs[1:] + list(arounds.values()) + list(sides.values()):
        copy.wait_send()


def per_device(activations, hidden_grad, routing, momentum, master):
    n_opt = lax.axis_size("opt")
    nz = lax.axis_size("dp") // NY
    outer = nz // INNER
    tokens, width = activations.shape
    top, hid = hidden_grad.shape[1:]
    quarter = width // NY
    group = NY * n_opt
    dma = pltpu.SemaphoreType.DMA
    shape = jax.ShapeDtypeStruct(momentum.shape[1:], f32)
    vmem = pl.BlockSpec(memory_space=pltpu.VMEM)
    result = pl.pallas_call(
        functools.partial(kernel, (nz, n_opt)),
        out_shape=jax.ShapeDtypeStruct((2, *shape.shape), f32),
        in_specs=[pl.BlockSpec(memory_space=pltpu.HBM)] * 4,
        out_specs=vmem,
        scratch_shapes=[
            pltpu.VMEM((tokens, width), bf16),
            pltpu.VMEM((tokens * top, hid), bf16),
            pltpu.VMEM((top, tokens), jnp.int32),
            pltpu.VMEM(shape.shape, f32),
            pltpu.VMEM((n_opt * CAP, tokens * top), bf16),
            pltpu.VMEM((n_opt, NY, CAP, quarter + hid), bf16),
            pltpu.VMEM((group, CAP, quarter + hid), bf16),
            pltpu.VMEM((INNER, outer, 8, hid), f32),
            pltpu.VMEM((3, outer, 8, hid), f32),
            pltpu.VMEM((outer, 8, hid), f32),
            pltpu.VMEM((outer, 8, hid), f32),
            pltpu.VMEM((NY * INNER, outer, 32, 128), jnp.int16),
            dma((4,)),
            dma,
            pltpu.SemaphoreType.REGULAR,
            pltpu.SemaphoreType.REGULAR,
            dma((group,)), dma((group,)),
            dma((3,)), dma((3,)),
            dma((outer,)), dma((outer,)),
            dma((outer,)), dma((outer,)),
            dma((INNER, len(GROUPS))), dma((INNER, len(GROUPS))),
            dma((NY * INNER, len(GROUPS))), dma((NY * INNER, len(GROUPS))),
        ],
        compiler_params=pltpu.CompilerParams(
            collective_id=0, has_side_effects=True, vmem_limit_bytes=60 * 1024 * 1024
        ),
    )(
        activations,
        hidden_grad.reshape(tokens * top, hid),
        routing.T,
        momentum[0],
    )
    new_moment, iterate = result[:1], result[1:]
    update = 0.2 * math.sqrt(max(width, hid)) * iterate
    master_out = (1.0 - learning_rate * weight_decay) * master - learning_rate * update
    return (new_moment, master_out, update)


def solution(mesh):
    placed = (
        P(("dp", "opt"), None),
        P(("dp", "opt"), None, None),
        P(("dp", "opt"), None),
        P("opt", "dp", None),
        P("opt", "dp", None),
    )
    return jax.shard_map(
        per_device,
        mesh=mesh,
        in_specs=placed,
        out_specs=(P("opt", "dp", None), P("opt", "dp", None), P("opt", "dp", None)),
        check_vma=False,
    )
```

```python
import functools
import math

import jax
import jax.numpy as jnp
from jax import lax
from jax.experimental import pallas as pl
from jax.experimental.pallas import tpu as pltpu
from jax.sharding import PartitionSpec as P

CAP = 32
NY = 4
INNER = 4
STRIDE = 5
MESH = pl.DeviceIdType.MESH

poly_first = 3.4445
poly_third = -4.775
poly_fifth = 2.0315
momentum_decay = 0.95
learning_rate = 0.02
weight_decay = 0.1
norm_epsilon = 1e-07

f32 = jnp.float32
bf16 = jnp.bfloat16


def halves(a):
    hi = a.astype(bf16)
    return hi, (a - hi.astype(f32)).astype(bf16)


def dot(a, b):
    return jnp.dot(a, b, preferred_element_type=f32)


def dot_t(a, b):
    return lax.dot_general(a, b, (((0,), (0,)), ((), ())), preferred_element_type=f32)


def dot3(a, b):
    (a_hi, a_lo), (b_hi, b_lo) = a, b
    return dot(a_hi, b_hi) + (dot(a_hi, b_lo) + dot(a_lo, b_hi))


def one_hot(cond):
    return jnp.where(cond, 1.0, 0.0).astype(bf16)


def step_of(exponent, mantissa):
    return mantissa * (jnp.exp2(exponent - 14.0) * (1 / 32767))


def coded(block):
    peak = jnp.maximum(jnp.max(jnp.abs(block), keepdims=True), 1e-30)
    exponent = jnp.floor(jnp.log(peak) * (1 / math.log(2)) + 0.001) + 1.0
    mantissa = jnp.floor(peak * jnp.exp2(14.0 - exponent)) + 2.0
    steps = jnp.round(block * (1.0 / step_of(exponent, mantissa)))
    parts = [steps[:, c : c + 128] for c in range(0, block.shape[1], 128)]
    first_half = lax.broadcasted_iota(jnp.int32, (8, 128), 0) < 4
    parts.append(jnp.where(first_half, exponent, mantissa))
    return jnp.concatenate(parts, axis=0).astype(jnp.int32).astype(jnp.int16)


def decoded(blocks):
    parts = blocks.astype(jnp.int32).astype(f32).reshape(-1, 4, 8, 128)
    step = step_of(parts[:, 3, 0:1], parts[:, 3, 4:5])
    return jnp.concatenate([(parts[:, c] * step).reshape(-1, 128) for c in range(3)], axis=1)


def running_count(flags):
    width = flags.shape[1]
    lane = lax.broadcasted_iota(jnp.int32, flags.shape, 1)
    total, shift = flags, 1
    while shift < width:
        total = total + jnp.where(lane >= shift, pltpu.roll(total, shift, 1), 0)
        shift *= 2
    return total


OFFSETS = (0, 1, 7, 2, 6, 3, 5, 4)
GROUPS = ((0, 3), (3, 5), (5, 8))
COLUMNS = (slice(0, 256), slice(256, 384))


def kernel(
    sizes,
    acts_hbm, hidden_hbm, names_hbm, momentum_hbm,
    result,
    acts, hidden, names, momentum,
    pick, send, recv, part, near, summed, far, rows,
    load_sem, local_sem, know_four, know_eight,
    go_send, go_recv, near_send, near_recv, far_send, far_recv,
    out_send, out_recv, around_send, around_recv, side_send, side_recv,
):
    nz, n_opt = sizes
    outer = nz // INNER
    dp, opt = lax.axis_index("dp"), lax.axis_index("opt")
    z, y = dp // NY, dp % NY
    cls, place = z % INNER, z // INNER
    width = acts.shape[1]
    quarter = width // NY
    hid = hidden.shape[1]
    group = NY * n_opt

    def at(zz, yy, oo):
        return (zz * NY + yy, oo)

    def offsets(i):
        r = i * STRIDE % group
        return r // n_opt, r % n_opt

    def go_peer(i):
        dy, do = offsets(i)
        return at(z, (y + dy) % NY, (opt + do) % n_opt)

    def along(dz):
        return at((z + nz + dz) % nz, y, opt)

    even = 1 - z % 2
    turn = 2 * even - (1 - even) * 2
    near_to = [along(1), along(-1), along(turn)]

    def far_to(q):
        return at((place + q) % outer * INNER + cls, y, opt)

    barrier = pltpu.get_barrier_semaphore()

    def greet(i, _):
        target = at(z, (y + NY // 2 + i // n_opt) % NY, (opt + n_opt // 2 + i % n_opt) % n_opt)
        pl.semaphore_signal(barrier, inc=1, device_id=target, device_id_type=MESH)
        return 0

    loads = [
        pltpu.make_async_copy(source, target, load_sem.at[i])
        for i, (source, target) in enumerate(
            [
                (names_hbm, names),
                (acts_hbm, acts),
                (hidden_hbm, hidden),
                (momentum_hbm, momentum),
            ]
        )
    ]
    own = NY // 2 * n_opt + n_opt // 2
    loads[0].start()
    for dz in (4, -4):
        pl.semaphore_signal(barrier, inc=1, device_id=along(dz), device_id_type=MESH)
    lax.fori_loop(0, own, greet, 0)
    for load in loads[1:]:
        load.start()
    lax.fori_loop(own + 1, group, greet, 0)
    for dz in (2, -2, 1, -1):
        pl.semaphore_signal(barrier, inc=1, device_id=along(dz), device_id_type=MESH)

    experts, tokens, top = n_opt, acts.shape[0], names.shape[0]
    spread_shape = (tokens, tokens * top)
    spread = one_hot(
        (lax.broadcasted_iota(jnp.int32, spread_shape, 1) >> (top.bit_length() - 1))
        == lax.broadcasted_iota(jnp.int32, spread_shape, 0)
    )
    loads[0].wait()
    expert = lax.broadcasted_iota(jnp.int32, (experts, tokens), 0)
    match = jnp.zeros((experts, tokens), jnp.int32)
    for k in range(top):
        match = match + (names[k : k + 1, :] == expert).astype(jnp.int32)
    per_token = jnp.where(match > 0, running_count(match) - 1, -1)
    both = jnp.concatenate([names[...], per_token], axis=0).astype(f32).astype(bf16)
    wide = dot(both, spread)
    slot = lax.broadcasted_iota(jnp.int32, (top, tokens * top), 1) & (top - 1)
    own_slot = slot == lax.broadcasted_iota(jnp.int32, slot.shape, 0)
    name = jnp.sum(jnp.where(own_slot, wide[:top], 0.0), axis=0, keepdims=True)
    expert = lax.broadcasted_iota(jnp.int32, (experts, tokens * top), 0).astype(f32)
    flat = jnp.where(name == expert, wide[top:], -1.0)
    for e in range(experts):
        j = lax.broadcasted_iota(jnp.int32, (CAP, flat.shape[1]), 0).astype(f32)
        pick[e * CAP : (e + 1) * CAP, :] = one_hot(flat[e : e + 1, :] == j)
    loads[2].wait()
    packed_grads = dot(pick[...], hidden[...]).astype(bf16)
    j = lax.broadcasted_iota(jnp.int32, (CAP, per_token.shape[1]), 0)
    pick_acts = jnp.concatenate([one_hot(per_token[e : e + 1, :] == j) for e in range(experts)], axis=0)
    loads[1].wait()
    packed_acts = dot(pick_acts, acts[...]).astype(bf16)
    parts = []
    row = lax.broadcasted_iota(jnp.int32, (quarter, quarter), 0)
    lane = lax.broadcasted_iota(jnp.int32, (quarter, quarter), 1)
    in_class = (((lane >> 3) & 1) * INNER + ((lane >> 4) & 3)) * (8 * NY) + (lane & 7)
    for i in range(NY):
        origin = in_class + ((((lane >> 6) + (NY - i)) & (NY - 1)) << 3)
        ordered = dot(packed_acts[:, i * quarter : (i + 1) * quarter], one_hot(row == origin))
        parts.append(ordered)
    low = (lax.broadcasted_iota(jnp.int32, (n_opt * CAP, 128), 1) & 64) == 0
    for q in range(NY):
        for half in range(2):
            lanes = slice(128 * half, 128 * half + 128)
            pieces = [parts[(2 * half + k + NY - q) % NY][:, lanes] for k in range(2)]
            piece = jnp.where(low, pieces[0], pieces[1]).astype(bf16)
            for e in range(experts):
                send[e, q, :, lanes] = piece[e * CAP : (e + 1) * CAP, :]
        for e in range(experts):
            send[e, q, :, quarter:] = packed_grads[e * CAP : (e + 1) * CAP, :]

    pl.semaphore_wait(barrier, group - 1 + 6)
    def go(i):
        dy, do = offsets(i)
        return pltpu.make_async_remote_copy(
            src_ref=send.at[(opt + do) % n_opt, (y + dy) % NY],
            dst_ref=recv.at[i],
            send_sem=go_send.at[i],
            recv_sem=go_recv.at[i],
            device_id=go_peer(i),
            device_id_type=MESH,
        )

    def start_go(r, _):
        go(r).start()
        return 0

    lax.fori_loop(1, group, start_go, 0)
    for dz in (4, -4):
        pl.semaphore_signal(know_four, inc=1, device_id=along(dz), device_id_type=MESH)
    own = pltpu.make_async_copy(send.at[opt, y], recv.at[0], local_sem)
    own.start()
    pl.semaphore_wait(know_four, 2)
    for dz in (8, -8):
        pl.semaphore_signal(know_eight, inc=1, device_id=along(dz), device_id_type=MESH)
    own.wait()

    def wait_go(r, _):
        go(r).wait_recv()
        return 0

    total = jnp.zeros((quarter, hid), f32)
    for begin, end in ((0, 8), (8, 16), (16, 24), (24, 28), (28, 32)):
        lax.fori_loop(max(1, begin), end, wait_go, 0)
        block = recv[begin:end].reshape((end - begin) * CAP, quarter + hid)
        total = total + dot_t(block[:, :quarter], block[:, quarter:])
    for p in range(NY):
        for c in range(INNER):
            rows_at = p * 64 + c * 16
            pair = pl.ds(2 * ((p + NY - y) % NY), 2)
            part[c, pair] = total[rows_at : rows_at + 16].reshape(2, 8, hid)

    steps = (1, INNER - 1, 2)
    nears, fars = {}, {}
    for h, cols in enumerate(COLUMNS):
        for s in range(3):
            nears[h, s] = pltpu.make_async_remote_copy(
                src_ref=part.at[(cls + steps[s]) % INNER, :, :, cols],
                dst_ref=near.at[s, :, :, cols],
                send_sem=near_send.at[h, s],
                recv_sem=near_recv.at[h, s],
                device_id=near_to[s],
                device_id_type=MESH,
            )
            nears[h, s].start()
    pl.semaphore_wait(know_eight, 2)
    for h, cols in enumerate(COLUMNS):
        for s in range(3):
            nears[h, s].wait_recv()
        summed[:, :, cols] = part[cls, :, :, cols] + (
            near[0, :, :, cols] + (near[1, :, :, cols] + near[2, :, :, cols])
        )
        for q in OFFSETS[:0:-1]:
            fars[h, q] = pltpu.make_async_remote_copy(
                src_ref=summed.at[(place + q) % outer, :, cols],
                dst_ref=far.at[q, :, cols],
                send_sem=far_send.at[h, q],
                recv_sem=far_recv.at[h, q],
                device_id=far_to(q),
                device_id_type=MESH,
            )
            fars[h, q].start()
    loads[3].wait()
    grad = summed[place]
    for q in OFFSETS[1:]:
        for h in range(len(COLUMNS)):
            fars[h, q].wait_recv()
        grad = grad + far[q]
    moment = momentum_decay * momentum[...] + grad
    result[0] = moment

    rows[0, 0] = coded(moment)
    outs = [None] * outer
    for i in range(outer - 1, 0, -1):
        outs[i] = pltpu.make_async_remote_copy(
            src_ref=rows.at[0, 0],
            dst_ref=rows.at[0, i],
            send_sem=out_send.at[i],
            recv_sem=out_recv.at[i],
            device_id=far_to(OFFSETS[i]),
            device_id_type=MESH,
        )
        outs[i].start()
    arounds, sides = {}, {}

    def to_sides(s, g):
        begin, end = GROUPS[g]
        for d in range(1, NY):
            slot = d * INNER + s
            sides[slot, g] = pltpu.make_async_remote_copy(
                src_ref=rows.at[s, begin:end],
                dst_ref=rows.at[slot, begin:end],
                send_sem=side_send.at[slot, g],
                recv_sem=side_recv.at[slot, g],
                device_id=at(z, (y + d) % NY, opt),
                device_id_type=MESH,
            )
            sides[slot, g].start()

    def from_places(g):
        begin, end = GROUPS[g]
        for i in range(max(begin, 1), end):
            outs[i].wait_recv()
        for s in range(1, INNER):
            arounds[s, g] = pltpu.make_async_remote_copy(
                src_ref=rows.at[0, begin:end],
                dst_ref=rows.at[s, begin:end],
                send_sem=around_send.at[s, g],
                recv_sem=around_recv.at[s, g],
                device_id=near_to[s - 1],
                device_id_type=MESH,
            )
            arounds[s, g].start()
        to_sides(0, g)

    def from_classes(g):
        for s in range(1, INNER):
            arounds[s, g].wait_recv()
            to_sides(s, g)

    last = len(GROUPS)
    for g in range(last + 1):
        if g < last:
            from_places(g)
        if g > 0:
            from_classes(g - 1)
    gram_hi = jnp.zeros((hid, hid), f32)
    gram_lo = jnp.zeros((hid, hid), f32)
    for g, (begin, end) in enumerate(GROUPS):
        for slot in range(INNER, NY * INNER):
            sides[slot, g].wait_recv()
        hi, lo = halves(decoded(rows[:, begin:end]))
        gram_hi, gram_lo = gram_hi + dot_t(hi, hi), gram_lo + dot_t(hi, lo)

    gram = gram_hi + (gram_lo + gram_lo.T)
    eye = lax.broadcasted_iota(jnp.int32, gram.shape, 0) == lax.broadcasted_iota(jnp.int32, gram.shape, 1)
    scale = lax.rsqrt(jnp.sum(jnp.where(eye, gram, 0.0)) + norm_epsilon)
    one = jnp.where(eye, poly_first, 0.0)
    gram = gram * (scale * scale)
    gram_parts = halves(gram)
    first = one + (poly_third * gram + poly_fifth * dot3(gram_parts, gram_parts))
    first_parts = halves(first)
    later = dot3(first_parts, halves(dot3(gram_parts, first_parts)))
    later_parts = halves(later)
    second = one + (poly_third * later + poly_fifth * dot3(later_parts, later_parts))
    result[1] = dot3(halves(dot3(halves(moment * scale), first_parts)), halves(second))

    def wait_sent(i, _):
        go(i).wait_send()
        return 0

    lax.fori_loop(1, group, wait_sent, 0)
    for copy in [*nears.values(), *fars.values(), *outs[1:], *arounds.values(), *sides.values()]:
        copy.wait_send()


def per_device(activations, hidden_grad, routing, momentum, master):
    n_opt = lax.axis_size("opt")
    nz = lax.axis_size("dp") // NY
    outer = nz // INNER
    tokens, width = activations.shape
    top, hid = hidden_grad.shape[1:]
    quarter = width // NY
    group = NY * n_opt
    dma = pltpu.SemaphoreType.DMA
    shape = jax.ShapeDtypeStruct(momentum.shape[1:], f32)
    vmem = pl.BlockSpec(memory_space=pltpu.VMEM)
    result = pl.pallas_call(
        functools.partial(kernel, (nz, n_opt)),
        out_shape=jax.ShapeDtypeStruct((2, *shape.shape), f32),
        in_specs=[pl.BlockSpec(memory_space=pltpu.HBM)] * 4,
        out_specs=vmem,
        scratch_shapes=[
            pltpu.VMEM((tokens, width), bf16),
            pltpu.VMEM((tokens * top, hid), bf16),
            pltpu.VMEM((top, tokens), jnp.int32),
            pltpu.VMEM(shape.shape, f32),
            pltpu.VMEM((n_opt * CAP, tokens * top), bf16),
            pltpu.VMEM((n_opt, NY, CAP, quarter + hid), bf16),
            pltpu.VMEM((group, CAP, quarter + hid), bf16),
            pltpu.VMEM((INNER, outer, 8, hid), f32),
            pltpu.VMEM((3, outer, 8, hid), f32),
            pltpu.VMEM((outer, 8, hid), f32),
            pltpu.VMEM((outer, 8, hid), f32),
            pltpu.VMEM((NY * INNER, outer, 32, 128), jnp.int16),
            dma((4,)),
            dma,
            pltpu.SemaphoreType.REGULAR,
            pltpu.SemaphoreType.REGULAR,
            dma((group,)), dma((group,)),
            dma((len(COLUMNS), 3)), dma((len(COLUMNS), 3)),
            dma((len(COLUMNS), outer)), dma((len(COLUMNS), outer)),
            dma((outer,)), dma((outer,)),
            dma((INNER, len(GROUPS))), dma((INNER, len(GROUPS))),
            dma((NY * INNER, len(GROUPS))), dma((NY * INNER, len(GROUPS))),
        ],
        compiler_params=pltpu.CompilerParams(
            collective_id=0, has_side_effects=True, vmem_limit_bytes=60 * 1024 * 1024
        ),
    )(
        activations,
        hidden_grad.reshape(tokens * top, hid),
        routing.T,
        momentum[0],
    )
    new_moment, iterate = result[:1], result[1:]
    update = 0.2 * math.sqrt(max(width, hid)) * iterate
    master_out = (1.0 - learning_rate * weight_decay) * master - learning_rate * update
    return (new_moment, master_out, update)


def solution(mesh):
    placed = (
        P(("dp", "opt"), None),
        P(("dp", "opt"), None, None),
        P(("dp", "opt"), None),
        P("opt", "dp", None),
        P("opt", "dp", None),
    )
    return jax.shard_map(
        per_device,
        mesh=mesh,
        in_specs=placed,
        out_specs=(P("opt", "dp", None), P("opt", "dp", None), P("opt", "dp", None)),
        check_vma=False,
    )
```
